512 devices in a mesh: tok: 32 (over z, core), batch: 16 (over y, x).
Axes of the slice: x: 4, y: 4, z: 16, core: 2. Of those that a mesh axis runs over, the one named last changes fastest.
Arguments:
- table: bfloat16 [524288, 256], P(('tok', 'batch')), may hold values from -6 to 6
- hist_owner: int32 [2048, 128, 1], P(('batch', 'tok')), may hold values from 0 to 511; in each aligned block of 512 rows (0 to 511, 512 to 1023, ..., all dimensions but the last counted through in order) at most 2 rows name the same one
- hist_row: int32 [2048, 128], P(('batch', 'tok')), may hold values from 0 to 1023
- hist_len: int32 [2048], P(('batch', 'tok')), may hold values from 1 to 128, 131072 in all
- w_in: bfloat16 [256, 1024], replicated, may hold values from -0.375 to 0.375
- queries: bfloat16 [64, 1024], replicated, may hold values from -1200 to 1200
- ffn_gain: float32 [64, 1024], P('tok'), may hold values from 0.1 to 1.9
- w_gate: bfloat16 [64, 1024, 768], P('tok', 'batch'), may hold values from -0.1875 to 0.1875
- w_up: bfloat16 [64, 1024, 768], P('tok', 'batch'), may hold values from -0.1875 to 0.1875
- w_down: bfloat16 [64, 768, 1024], P('tok', 'batch'), may hold values from -0.21875 to 0.21875
Outputs:
- tokens_out: bfloat16 [2048, 64, 1024], P('batch', 'tok')
The draws below stay inside these ranges and needn't reach their ends.
Inputs may be any that keep to these rules, and one draw needn't show every extreme that they name: `hist_owner`: among the 512 slots of the users of one device, no owner is named more than 2 times, a bound that some block reaches.
All inputs are finite; a program needn't handle non-finite values. No bound on the sum of `hist_len` on one device may be relied on, other than what follows from the above.
Results may differ from the reference program's by a relative error of at most 0.019.
The reference program's roundings to bfloat16 on the way (of `rows`, `keys`, `attn`, `pooled`, `mixed`, `normed`, `hidden` and `summed`) count: a program that leaves them out, or rounds other values in their place, can miss the bound.
Values may be sent and summed in bfloat16 or wider, within the bound.
No kernel may reach another device: no remote copies, remote signals or barrier semaphores. Data moves between devices by JAX's collectives and lax.ppermute only.
A program may use at most 64 MiB of HBM per device.

```python
import math
import jax
import jax.numpy as jnp
import numpy as np
from jax import lax

EMB = 256
NQ = 64
HEAD = 16
FF = 768
HIST = 128
U_DEV = 4
ROWS_DEV = 1024
D = 1024
USERS = 2048
ROWS = 524288
CAP = 2
DEVICES = 512


def draw_queries(key, part):
    key = jax.random.fold_in(key, 7)
    base_key = jax.random.fold_in(key, 0)
    base = jnp.clip(jax.random.normal(base_key, (NQ, D), jnp.float32), -6.0, 6.0)
    return base.astype(jnp.bfloat16)


def touch_ends(result, own_key, low, largest):
    extent = result.shape
    spot = [jax.random.randint(jax.random.fold_in(own_key, axis), (), 0, extent[axis]) for axis in range(len(extent))]
    result = result.at[tuple(spot)].set(low)
    longest = extent.index(max(extent))
    spot[longest] = (spot[longest] + 1) % extent[longest]
    return result.at[tuple(spot)].set(largest)


def block_levels(own_key, dims, pieces, smallest, largest):
    loudness = 1.0
    for axis_at, blocks in pieces:
        steps = jax.random.uniform(jax.random.fold_in(jax.random.fold_in(own_key, 6), axis_at), (blocks,), jnp.float32, smallest / len(pieces), largest / len(pieces))
        loudness = loudness * jnp.repeat(jnp.exp(steps), dims[axis_at] // blocks).reshape((-1,) + (1,) * (len(dims) - 1 - axis_at))
    return loudness


def split_up(number_of, total, reach, skew):
    portions = [(1 << 20) // math.isqrt(standing ** skew) + 1 for standing in range(2, number_of + 1)]
    spare, counts = total - reach - (number_of - 1), [1] * (number_of - 1)
    while spare > 0:
        candidates = [i for i in range(number_of - 1) if counts[i] < reach]
        whole, remaining = sum([portions[i] for i in candidates]), spare
        for i in candidates:
            extra = min(reach - counts[i], max(1, remaining * portions[i] // whole), spare)
            counts[i] = counts[i] + extra
            spare = spare - extra
    return np.array([reach] + counts)


def ragged_sizes(own_key, number_of, total, limit, skew):
    if number_of == 2:
        one = jax.random.randint(own_key, (), max(1, total - limit), min(limit, total - 1) + 1)
        return jnp.stack([one, total - one])
    tallies = jnp.asarray(split_up(number_of, total, limit, skew), jnp.int32)
    pairs = (number_of - 1) // 2
    giver, sink = tallies[1:1 + 2 * pairs:2], tallies[2:2 + 2 * pairs:2]
    slack = jnp.minimum(giver - 1, limit - sink)
    shifted = jax.random.randint(jax.random.fold_in(own_key, 1), (pairs,), 0, 1 << 20) % (slack + 1)
    tallies = tallies.at[1:1 + 2 * pairs:2].set(giver - shifted).at[2:2 + 2 * pairs:2].set(sink + shifted)
    return tallies[jax.random.permutation(jax.random.fold_in(own_key, 2), number_of)]


def assign_block(key, own, number, rows, number_of, top, most, lean):
    order = jax.random.permutation(key, number_of)
    crowded, usual = portions_of(number_of, rows * top, most, lean, True), portions_of(number_of, rows * top, most, lean, False)
    places = jnp.arange(number_of)

    def named(lengths, offset_by):
        used = int((lengths > 0).sum())
        fixed = max(1, used // 4)
        moved = fixed + (places - fixed + offset_by * (used - fixed)) % max(1, number_of - fixed)
        return jnp.zeros((number_of,), jnp.int32).at[order[jnp.where(places < fixed, places, moved)]].set(jnp.asarray(lengths, jnp.int32))

    lengths = jnp.where(number % 4 == 0, named(crowded, number // 4), named(usual, number - number // 4 - 1))
    mixed = jax.random.permutation(jax.random.fold_in(own, 3), number_of)
    donor, sink = mixed[0:number_of // 2 * 2:2], mixed[1:number_of // 2 * 2:2]
    margin = jnp.minimum(lengths[donor] - 1, most - lengths[sink]) // 2
    margin = jnp.where((donor == order[0]) | (sink == order[0]) | (lengths[sink] == 0), 0, jnp.maximum(margin, 0))
    moved = jax.random.randint(jax.random.fold_in(own, 4), (number_of // 2,), 0, 1 << 20) % (margin + 1)
    lengths = lengths.at[donor].add(-moved).at[sink].add(moved)
    labels = jnp.searchsorted(jnp.cumsum(lengths), jnp.arange(rows * top), side="right").astype(jnp.int32)
    grid = labels.reshape(top, rows).T
    grid = grid[jax.random.permutation(jax.random.fold_in(own, 1), rows)]
    offset_by = jax.random.randint(jax.random.fold_in(own, 2), (rows, 1), 0, top)
    return jnp.take_along_axis(grid, (jnp.arange(top)[None, :] + offset_by) % top, axis=1)


def portions_of(count, total, bound, slope, full):
    loads = [(1 << 20) // math.isqrt(standing ** slope) + 1 for standing in range(1, count + 1)]
    largest = bound if full else min(bound, max(-(-total // count), total * loads[0] // sum(loads)))
    least = 1 if total - largest >= count - 1 else 0
    holding, rest = [largest] + [least] * (count - 1), total - largest - least * (count - 1)
    while rest > 0:
        movable = [i for i in range(1, count) if holding[i] < largest] or [i for i in range(1, count) if holding[i] < bound]
        pool, remaining = sum([loads[i] for i in movable]), rest
        for i in movable:
            more = min(bound - holding[i], max(1, remaining * loads[i] // pool), rest)
            holding[i] = holding[i] + more
            rest = rest - more
    return np.array(holding)


def centred(rng, extent, scale, reach, shards=(), kind=jnp.bfloat16):
    values = jax.random.normal(rng, extent, jnp.float32) * scale
    if len(shards) > 0:
        values = block_levels(rng, extent, shards, -0.22, 0.18) * values
    return jnp.clip(values, min=-reach, max=reach).astype(kind)


def setup_inputs(seed: int = 0) -> dict:
    splits = jax.random.split(jax.random.key(seed), 11)
    table = centred(splits[0], (ROWS, EMB), 1.0, 6.0, ((0, 512),))
    hist_owner_keys = jax.random.split(jax.random.fold_in(splits[1], 1), USERS * HIST // (U_DEV * HIST))
    hist_owner_turns = jax.random.permutation(jax.random.fold_in(splits[1], 3), USERS * HIST // (U_DEV * HIST))
    hist_owner = jax.vmap(lambda own, number: assign_block(jax.random.fold_in(splits[1], 2), own, number, U_DEV * HIST, DEVICES, 1, CAP, 2))(hist_owner_keys, hist_owner_turns).reshape((USERS, HIST, 1))
    hist_row = touch_ends(jax.random.randint(splits[2], (USERS, HIST), 0, ROWS_DEV), jax.random.fold_in(splits[2], 1), 0, ROWS_DEV - 1).astype(jnp.int32)
    hist_len = ragged_sizes(splits[3], USERS, USERS * HIST // 2, HIST, 2).astype(jnp.int32)
    w_in = centred(splits[4], (EMB, D), EMB ** -0.5, 0.375)
    queries = draw_queries(jax.random.fold_in(splits[10], 71), 0)
    ffn_gain = jnp.clip(1.0 + 0.18 * jax.random.normal(splits[6], (NQ, D), jnp.float32), 0.1, 1.9)
    w_gate = centred(splits[7], (NQ, D, FF), D ** -0.5, 0.1875, ((0, 32), (1, 16)))
    w_up = centred(splits[8], (NQ, D, FF), D ** -0.5, 0.1875, ((0, 32), (1, 16)))
    w_down = centred(splits[9], (NQ, FF, D), FF ** -0.5, 0.21875, ((0, 32), (1, 16)))
    return {"table": table, "hist_owner": hist_owner, "hist_row": hist_row, "hist_len": hist_len, "w_in": w_in, "queries": queries, "ffn_gain": ffn_gain, "w_gate": w_gate, "w_up": w_up, "w_down": w_down}


def rms_scale(values):
    return lax.rsqrt(lax.optimization_barrier(jnp.mean(values * values, axis=-1, keepdims=True)) + 1e-06)

def pool_block(table, owner_block, row_block, len_block, w_in, queries):
    index = owner_block[:, :, 0] * ROWS_DEV + row_block
    rows = jnp.take(table, index.reshape(-1).astype(jnp.int32), axis=0)
    proj = jnp.dot(rows, w_in, preferred_element_type=jnp.float32)
    keys = (proj * rms_scale(proj)).astype(jnp.bfloat16)
    users = owner_block.shape[0]
    keys = keys.reshape(users, HIST, NQ, HEAD).astype(jnp.float32)
    query_heads = queries.reshape(NQ, NQ, HEAD).astype(jnp.float32)
    scores = jnp.einsum('qhe,ujhe->uqhj', query_heads, keys) / jnp.sqrt(jnp.float32(HEAD))
    valid = jnp.arange(HIST)[None, :] < len_block[:, None]
    scores = jnp.where(valid[:, None, None, :], scores, jnp.float32(-1e+30))
    attn = jax.nn.softmax(scores, axis=-1).astype(jnp.bfloat16)
    pooled = jnp.einsum('uqhj,ujhe->uqhe', attn.astype(jnp.float32), keys)
    return pooled.astype(jnp.bfloat16).reshape(users, NQ, D)

def token_net(args):
    mixed_h, gain_h, gate_w, up_w, down_w = args
    wide = mixed_h.astype(jnp.float32)
    normed = (wide * rms_scale(wide) * gain_h[None, :]).astype(jnp.bfloat16)
    gate = jnp.dot(normed, gate_w, preferred_element_type=jnp.float32)
    up_val = jnp.dot(normed, up_w, preferred_element_type=jnp.float32)
    hidden = (jax.nn.silu(gate) * up_val).astype(jnp.bfloat16)
    down = jnp.dot(hidden, down_w, preferred_element_type=jnp.float32)
    return (wide + down).astype(jnp.bfloat16)

def reference(table, hist_owner, hist_row, hist_len, w_in, queries, ffn_gain, w_gate, w_up, w_down):
    blocks = USERS // U_DEV

    def one_block(args):
        owner_block, row_block, len_block = args
        return pool_block(table, owner_block, row_block, len_block, w_in, queries)
    pooled = lax.map(one_block, (hist_owner.reshape(blocks, U_DEV, HIST, 1), hist_row.reshape(blocks, U_DEV, HIST), hist_len.reshape(blocks, U_DEV)))
    pooled = pooled.reshape(USERS, NQ, NQ, HEAD)
    mixed = pooled.transpose(2, 0, 1, 3).reshape(NQ, USERS, D)
    summed = lax.map(token_net, (mixed, ffn_gain, w_gate, w_up, w_down))
    return summed.reshape(NQ, USERS, NQ, HEAD).transpose(1, 2, 0, 3).reshape(USERS, NQ, D)
```

```python
import jax
import jax.numpy as jnp
from jax import lax
from jax.experimental import pallas as pl
from jax.experimental.pallas import tpu as pltpu
from jax.sharding import PartitionSpec as P

HEADS_STEP = 8
MASKED = -1e30
EPS = 1e-06
VMEM_BYTES = 50 * 1024 * 1024


def dot32(left, right):
    return jnp.dot(left, right, preferred_element_type=jnp.float32)


def one_hot(index, width):
    lanes = lax.broadcasted_iota(jnp.int32, (index.shape[0], width), 1)
    return jnp.where(lanes == index, 1.0, 0.0).astype(jnp.bfloat16)


def pool_kernel(len_ref, answer_ref, position_ref, w_in_ref, query_ref, out_ref, keys_ref):
    users = len_ref.shape[0]
    slots = position_ref.shape[0] // users
    steps = keys_ref.shape[0]
    step_width = keys_ref.shape[2]
    headsz = step_width // HEADS_STEP
    nquery = query_ref.shape[2]
    step = pl.program_id(0)

    @pl.when(step == 0)
    def _():
        for user in range(users):
            span = slice(user * slots, (user + 1) * slots)
            pick = one_hot(position_ref[span, :], answer_ref.shape[0])
            rows = dot32(pick, answer_ref[...]).astype(jnp.bfloat16)
            proj = dot32(rows, w_in_ref[...])
            scale = lax.rsqrt(jnp.mean(proj * proj, axis=-1, keepdims=True) + EPS)
            keys = (proj * scale).astype(jnp.bfloat16)
            for part in range(steps):
                keys_ref[part, span, :] = keys[:, part * step_width : (part + 1) * step_width]

    query = query_ref[0].astype(jnp.float32)
    wide = jnp.concatenate([query] * HEADS_STEP, axis=1)
    row_head = lax.broadcasted_iota(jnp.int32, wide.shape, 0) // headsz
    col_head = lax.broadcasted_iota(jnp.int32, wide.shape, 1) // nquery
    spread = jnp.where(row_head == col_head, wide, 0.0).astype(jnp.bfloat16)
    half_heads = HEADS_STEP // 2
    blocks = {}
    for user in range(users):
        keys = keys_ref[step, user * slots : (user + 1) * slots, :]
        scores = dot32(keys, spread)
        slot = lax.broadcasted_iota(jnp.int32, scores.shape, 0)
        scores = jnp.where(slot < len_ref[user], scores, MASKED)
        top = jnp.max(scores, axis=0, keepdims=True)
        weight = jnp.exp((scores - top) * (1.0 / headsz**0.5))
        total = jnp.sum(weight, axis=0, keepdims=True)
        attn = (weight * (1.0 / total)).astype(jnp.bfloat16)
        keys_t = keys.astype(jnp.float32).T.astype(jnp.bfloat16)
        for half in range(2):
            rows = keys_t[half * half_heads * headsz : (half + 1) * half_heads * headsz, :]
            cols = attn[:, half * half_heads * nquery : (half + 1) * half_heads * nquery]
            pooled = dot32(rows, cols)
            for head in range(half_heads):
                block = pooled[
                    head * headsz : (head + 1) * headsz, head * nquery : (head + 1) * nquery
                ]
                low = block[: headsz // 2, :]
                high = block[headsz // 2 :, :]
                blocks[user, half * half_heads + head] = jnp.concatenate([low, high], axis=1)
    for pair in range(HEADS_STEP // 2):
        stack = jnp.stack(
            [blocks[user, 2 * pair + which] for user in range(users) for which in range(2)], axis=0
        )
        turned = jnp.swapaxes(stack, 0, 1)
        row = jnp.concatenate([turned[part] for part in range(turned.shape[0])], axis=1)
        out_ref[pair, :, :] = row.astype(jnp.bfloat16)


def pool(lengths, answers, position, w_in, queries):
    users = lengths.shape[0]
    width = w_in.shape[1]
    nquery = queries.shape[0]
    headsz = width // nquery
    steps = nquery // HEADS_STEP
    step_width = width // steps
    query_t = queries.T.reshape(steps, step_width, nquery)
    pairs = nquery // 2
    return pl.pallas_call(
        pool_kernel,
        grid=(steps,),
        in_specs=[
            pl.BlockSpec(memory_space=pltpu.SMEM),
            pl.BlockSpec(answers.shape, lambda i: (0, 0)),
            pl.BlockSpec(position.shape, lambda i: (0, 0)),
            pl.BlockSpec(w_in.shape, lambda i: (0, 0)),
            pl.BlockSpec((1, step_width, nquery), lambda i: (i, 0, 0)),
        ],
        out_specs=pl.BlockSpec((HEADS_STEP // 2, 2 * users, width), lambda i: (i, 0, 0)),
        out_shape=jax.ShapeDtypeStruct((pairs, 2 * users, width), jnp.bfloat16),
        scratch_shapes=[pltpu.VMEM((steps, position.shape[0], step_width), jnp.bfloat16)],
        compiler_params=pltpu.CompilerParams(vmem_limit_bytes=VMEM_BYTES),
    )(lengths, answers, position, w_in, query_t)


def net_kernel(mixed_ref, gain_ref, weight_ref, out_ref, gate_ref, up_ref, down_ref, sems):
    tokens = gain_ref.shape[0]
    rows, width = mixed_ref.shape
    group = rows // tokens
    nparts, _, part_rows, hidden_width = weight_ref.shape
    down_rows = down_ref.shape[2]
    rest = width - hidden_width
    headsz = out_ref.shape[3]
    copies = []
    for token in range(tokens):
        pieces = [
            (weight_ref.at[:, token, :, :], gate_ref.at[token]),
            (weight_ref.at[:, tokens + token, :, :], up_ref.at[token]),
            (
                weight_ref.at[:, 2 * tokens + token, pl.ds(0, down_rows), :],
                down_ref.at[token, :, :, pl.ds(0, hidden_width)],
            ),
        ]
        extra = part_rows - down_rows
        for piece in range(down_rows // extra):
            pieces.append(
                (
                    weight_ref.at[
                        :, 2 * tokens + token, pl.ds(down_rows, extra), pl.ds(piece * rest, rest)
                    ],
                    down_ref.at[token, :, pl.ds(piece * extra, extra), pl.ds(hidden_width, rest)],
                )
            )
        copies.append(
            [
                pltpu.make_async_copy(src, dst, sems.at[token, number])
                for number, (src, dst) in enumerate(pieces)
            ]
        )
    for some in copies:
        for copy in some:
            copy.start()
    target = lax.broadcasted_iota(jnp.int32, (rows, 1), 0)
    order = (target % group) * tokens + target // group
    sorted_rows = dot32(one_hot(order, rows), mixed_ref[...]).astype(jnp.bfloat16)
    nquery = width // headsz
    spot = lax.broadcasted_iota(jnp.int32, (width, 1), 0)
    feature = spot % nquery * headsz + (spot // nquery % 2) * (headsz // 2) + spot // (2 * nquery)
    mixed = dot32(sorted_rows, one_hot(feature, width))
    for token in range(tokens):
        wide = mixed[token * group : (token + 1) * group, :]
        scale = lax.rsqrt(jnp.mean(wide * wide, axis=-1, keepdims=True) + EPS)
        normed = (wide * scale * gain_ref[token : token + 1, :]).astype(jnp.bfloat16)
        copies[token][0].wait()
        gate = dot32(normed, gate_ref[token].reshape(width, hidden_width))
        copies[token][1].wait()
        up_val = dot32(normed, up_ref[token].reshape(width, hidden_width))
        hidden = (gate / (1.0 + jnp.exp(-gate)) * up_val).astype(jnp.bfloat16)
        for copy in copies[token][2:]:
            copy.wait()
        down = dot32(hidden, down_ref[token].reshape(hidden_width, width))
        summed = (wide + down).T.astype(jnp.bfloat16)
        out_ref[:, :, token, :, :] = summed.reshape(
            out_ref.shape[0], out_ref.shape[1], headsz, group
        )


def net(mixed, gain, weights, ntok):
    rows, width = mixed.shape
    tokens = gain.shape[0]
    group = rows // tokens
    nparts, _, part_rows, hidden_width = weights.shape
    down_rows = hidden_width // nparts
    nquery = ntok * tokens
    pieces = 3 + down_rows // (part_rows - down_rows)
    return pl.pallas_call(
        net_kernel,
        in_specs=[
            pl.BlockSpec(memory_space=pltpu.VMEM),
            pl.BlockSpec(memory_space=pltpu.VMEM),
            pl.BlockSpec(memory_space=pl.ANY),
        ],
        out_specs=pl.BlockSpec(memory_space=pltpu.VMEM),
        out_shape=jax.ShapeDtypeStruct(
            (ntok, tokens, tokens, width // nquery, group), jnp.bfloat16
        ),
        scratch_shapes=[
            pltpu.VMEM((tokens, nparts, part_rows, hidden_width), jnp.bfloat16),
            pltpu.VMEM((tokens, nparts, part_rows, hidden_width), jnp.bfloat16),
            pltpu.VMEM((tokens, nparts, down_rows, width), jnp.bfloat16),
            pltpu.SemaphoreType.DMA((tokens, pieces)),
        ],
        compiler_params=pltpu.CompilerParams(vmem_limit_bytes=VMEM_BYTES),
    )(mixed, gain, weights)


def pack_weights(w_gate, w_up, w_down):
    hidden_width = w_gate.shape[2]
    rest = w_down.shape[2] - hidden_width
    extra = w_gate.shape[1] - w_down.shape[1]
    pieces = [
        w_down[:, at : at + extra, hidden_width:] for at in range(0, w_down.shape[1], extra)
    ]
    tail = jnp.concatenate(pieces, axis=2)
    down = jnp.concatenate([w_down[:, :, :hidden_width], tail], axis=1)
    return jnp.concatenate([w_gate, w_up, down], axis=0)


def shards(table, hist_owner, hist_row, hist_len, w_in, queries, ffn_gain, w_gate, w_up, w_down):
    ntok = lax.axis_size("tok")
    nbatch = lax.axis_size("batch")
    devices = ntok * nbatch
    users, slots = hist_row.shape
    emb = table.shape[1]
    width = w_in.shape[1]
    nquery = queries.shape[0]
    headsz = width // nquery
    count = users * slots
    cap = 2 * count // devices
    weights = lax.all_gather(pack_weights(w_gate, w_up, w_down)[None], "batch", axis=0, tiled=True)

    owners = hist_owner.reshape(count)
    places = jnp.arange(count, dtype=jnp.int32)
    same = (owners[:, None] == owners[None, :]) & (places[None, :] < places[:, None])
    rank = jnp.sum(same.astype(jnp.int32), axis=1)
    position = owners * cap + rank
    spots = jnp.arange(devices * cap, dtype=jnp.int32)
    request = jnp.sum(
        jnp.where(position[:, None] == spots[None, :], hist_row.reshape(count)[:, None], 0), axis=0
    )
    asked = lax.all_to_all(request.reshape(ntok, nbatch * cap), "tok", 0, 0, tiled=True)
    asked = asked.reshape(ntok, nbatch, cap).transpose(1, 0, 2).reshape(nbatch, ntok * cap)
    asked = lax.all_to_all(asked, "batch", 0, 0, tiled=True)
    wanted = asked.reshape(nbatch, ntok, cap).transpose(1, 0, 2).reshape(devices * cap)
    local = jnp.arange(table.shape[0], dtype=jnp.int32)
    served = jnp.dot(
        (wanted[:, None] == local[None, :]).astype(jnp.bfloat16),
        table,
        preferred_element_type=jnp.bfloat16,
    )
    answers = lax.all_to_all(
        served.reshape(devices, cap, emb), ("tok", "batch"), 0, 0, tiled=True
    ).reshape(devices * cap, emb)
    pooled = pool(hist_len, answers, position.reshape(count, 1), w_in, queries)
    mixed = lax.all_to_all(pooled, "tok", 0, 0, tiled=True)
    group = users * ntok
    tokens = nquery // ntok
    sent = net(mixed.reshape(group * tokens, width), ffn_gain, weights, ntok)
    back = lax.all_to_all(sent, "tok", 0, 0, tiled=True)
    return back.transpose(4, 1, 0, 2, 3).reshape(group, tokens, width)


def solution(mesh):
    placed = (
        P(("tok", "batch"), None),
        P(("batch", "tok"), None, None),
        P(("batch", "tok"), None),
        P(("batch", "tok")),
        P(),
        P(),
        P("tok", None),
        P("tok", "batch", None),
        P("tok", "batch", None),
        P("tok", "batch", None),
    )
    return jax.shard_map(
        shards, mesh=mesh, in_specs=placed, out_specs=P("batch", "tok", None), check_vma=False
    )
```

```python
import jax
import jax.numpy as jnp
from jax import lax
from jax.experimental import pallas as pl
from jax.experimental.pallas import tpu as pltpu
from jax.sharding import PartitionSpec as P

HEADS_STEP = 8
INNER = 4
MASKED = -1e30
LOG2E = 1.4426950408889634
EPS = 1e-06
VMEM_BYTES = 50 * 1024 * 1024


def dot32(left, right):
    return jnp.dot(left, right, preferred_element_type=jnp.float32)


def one_hot(index, width):
    lanes = lax.broadcasted_iota(jnp.int32, (index.shape[0], width), 1)
    return jnp.where(lanes == index, 1.0, 0.0).astype(jnp.bfloat16)


def pool_kernel(len_ref, answer_ref, position_ref, w_in_ref, query_ref, out_ref, keys_ref):
    users = len_ref.shape[0]
    slots = position_ref.shape[0] // users
    inner, step_width, nquery = query_ref.shape
    headsz = step_width // HEADS_STEP
    heads = HEADS_STEP // 2
    step = pl.program_id(0)

    @pl.when(step == 0)
    def _():
        for user in range(users):
            span = slice(user * slots, (user + 1) * slots)
            pick = one_hot(position_ref[span, :], answer_ref.shape[0])
            rows = dot32(pick, answer_ref[...]).astype(jnp.bfloat16)
            proj = dot32(rows, w_in_ref[...])
            scale = lax.rsqrt(jnp.mean(proj * proj, axis=-1, keepdims=True) + EPS)
            keys = (proj * scale).astype(jnp.bfloat16)
            for part in range(keys_ref.shape[0]):
                keys_ref[part, span, :] = keys[:, part * step_width : (part + 1) * step_width]

    for sub in range(inner):
        query = query_ref[sub].astype(jnp.float32)
        wide = jnp.concatenate([query] * heads, axis=1)
        row_head = lax.broadcasted_iota(jnp.int32, wide.shape, 0) // headsz
        col_head = lax.broadcasted_iota(jnp.int32, wide.shape, 1) // nquery
        blocks = {}
        for half in range(2):
            spread = jnp.where(row_head == col_head + half * heads, wide, 0.0).astype(jnp.bfloat16)
            for user in range(users):
                keys = keys_ref[step * inner + sub, user * slots : (user + 1) * slots, :]
                scores = dot32(keys, spread)
                slot = lax.broadcasted_iota(jnp.int32, scores.shape, 0)
                scores = jnp.where(slot < len_ref[user], scores, MASKED)
                top = jnp.max(scores, axis=0, keepdims=True)
                weight = jnp.exp2((scores - top) * (LOG2E / headsz**0.5))
                total = jnp.sum(weight, axis=0, keepdims=True)
                attn = (weight * (1.0 / total)).astype(jnp.bfloat16)
                pooled = lax.dot_general(
                    keys, attn, (((0,), (0,)), ((), ())), preferred_element_type=jnp.float32
                )
                for head in range(heads):
                    at = (half * heads + head) * headsz
                    block = pooled[at : at + headsz, head * nquery : (head + 1) * nquery]
                    low = block[: headsz // 2, :]
                    high = block[headsz // 2 :, :]
                    blocks[user, half * heads + head] = jnp.concatenate([low, high], axis=1)
        for pair in range(heads):
            stack = jnp.stack(
                [blocks[user, 2 * pair + which] for user in range(users) for which in range(2)],
                axis=0,
            )
            turned = jnp.swapaxes(stack, 0, 1)
            row = jnp.concatenate([turned[part] for part in range(turned.shape[0])], axis=1)
            out_ref[sub * heads + pair, :, :] = row.astype(jnp.bfloat16)


def pool(lengths, answers, position, w_in, queries):
    users = lengths.shape[0]
    width = w_in.shape[1]
    nquery = queries.shape[0]
    parts = nquery // HEADS_STEP
    step_width = width // parts
    query_t = queries.T.reshape(parts, step_width, nquery)
    pairs = nquery // 2
    return pl.pallas_call(
        pool_kernel,
        grid=(parts // INNER,),
        in_specs=[
            pl.BlockSpec(memory_space=pltpu.SMEM),
            pl.BlockSpec(answers.shape, lambda i: (0, 0)),
            pl.BlockSpec(position.shape, lambda i: (0, 0)),
            pl.BlockSpec(w_in.shape, lambda i: (0, 0)),
            pl.BlockSpec((INNER, step_width, nquery), lambda i: (i, 0, 0)),
        ],
        out_specs=pl.BlockSpec((INNER * HEADS_STEP // 2, 2 * users, width), lambda i: (i, 0, 0)),
        out_shape=jax.ShapeDtypeStruct((pairs, 2 * users, width), jnp.bfloat16),
        scratch_shapes=[pltpu.VMEM((parts, position.shape[0], step_width), jnp.bfloat16)],
        compiler_params=pltpu.CompilerParams(vmem_limit_bytes=VMEM_BYTES),
    )(lengths, answers, position, w_in, query_t)


def net_kernel(mixed_ref, gain_ref, weight_ref, out_ref, gate_ref, up_ref, down_ref, sems):
    tokens = gain_ref.shape[0]
    rows, width = mixed_ref.shape
    group = rows // tokens
    nparts, _, part_rows, hidden_width = weight_ref.shape
    down_rows = down_ref.shape[2]
    rest = width - hidden_width
    headsz = out_ref.shape[3]
    copies = []
    for token in range(tokens):
        pieces = [
            (weight_ref.at[:, token, :, :], gate_ref.at[token]),
            (weight_ref.at[:, tokens + token, :, :], up_ref.at[token]),
            (
                weight_ref.at[:, 2 * tokens + token, pl.ds(0, down_rows), :],
                down_ref.at[token, :, :, pl.ds(0, hidden_width)],
            ),
        ]
        extra = part_rows - down_rows
        for piece in range(down_rows // extra):
            pieces.append(
                (
                    weight_ref.at[
                        :, 2 * tokens + token, pl.ds(down_rows, extra), pl.ds(piece * rest, rest)
                    ],
                    down_ref.at[token, :, pl.ds(piece * extra, extra), pl.ds(hidden_width, rest)],
                )
            )
        copies.append(
            [
                pltpu.make_async_copy(src, dst, sems.at[token, number])
                for number, (src, dst) in enumerate(pieces)
            ]
        )
    for some in copies:
        for copy in some:
            copy.start()
    target = lax.broadcasted_iota(jnp.int32, (rows, 1), 0)
    order = (target % group) * tokens + target // group
    sorted_rows = dot32(one_hot(order, rows), mixed_ref[...]).astype(jnp.bfloat16)
    nquery = width // headsz
    spot = lax.broadcasted_iota(jnp.int32, (width, 1), 0)
    feature = spot % nquery * headsz + (spot // nquery % 2) * (headsz // 2) + spot // (2 * nquery)
    mixed = dot32(sorted_rows, one_hot(feature, width))
    for token in range(tokens):
        wide = mixed[token * group : (token + 1) * group, :]
        scale = lax.rsqrt(jnp.mean(wide * wide, axis=-1, keepdims=True) + EPS)
        normed = (wide * scale * gain_ref[token : token + 1, :]).astype(jnp.bfloat16)
        copies[token][0].wait()
        gate = dot32(normed, gate_ref[token].reshape(width, hidden_width))
        copies[token][1].wait()
        up_val = dot32(normed, up_ref[token].reshape(width, hidden_width))
        hidden = (gate / (1.0 + jnp.exp(-gate)) * up_val).astype(jnp.bfloat16)
        for copy in copies[token][2:]:
            copy.wait()
        down = dot32(hidden, down_ref[token].reshape(hidden_width, width))
        summed = (wide + down).T.astype(jnp.bfloat16)
        out_ref[:, :, token, :, :] = summed.reshape(
            out_ref.shape[0], out_ref.shape[1], headsz, group
        )


def net(mixed, gain, weights, ntok):
    rows, width = mixed.shape
    tokens = gain.shape[0]
    group = rows // tokens
    nparts, _, part_rows, hidden_width = weights.shape
    down_rows = hidden_width // nparts
    nquery = ntok * tokens
    pieces = 3 + down_rows // (part_rows - down_rows)
    return pl.pallas_call(
        net_kernel,
        in_specs=[
            pl.BlockSpec(memory_space=pltpu.VMEM),
            pl.BlockSpec(memory_space=pltpu.VMEM),
            pl.BlockSpec(memory_space=pl.ANY),
        ],
        out_specs=pl.BlockSpec(memory_space=pltpu.VMEM),
        out_shape=jax.ShapeDtypeStruct(
            (ntok, tokens, tokens, width // nquery, group), jnp.bfloat16
        ),
        scratch_shapes=[
            pltpu.VMEM((tokens, nparts, part_rows, hidden_width), jnp.bfloat16),
            pltpu.VMEM((tokens, nparts, part_rows, hidden_width), jnp.bfloat16),
            pltpu.VMEM((tokens, nparts, down_rows, width), jnp.bfloat16),
            pltpu.SemaphoreType.DMA((tokens, pieces)),
        ],
        compiler_params=pltpu.CompilerParams(vmem_limit_bytes=VMEM_BYTES),
    )(mixed, gain, weights)


def pack_kernel(gate_ref, up_ref, down_ref, out_ref):
    tokens, part_rows, hidden_width = gate_ref.shape
    _, down_rows, width = down_ref.shape
    rest = width - hidden_width
    extra = part_rows - down_rows
    out_ref[:tokens] = gate_ref[...]
    out_ref[tokens : 2 * tokens] = up_ref[...]
    out_ref[2 * tokens :, :down_rows, :] = down_ref[:, :, :hidden_width]
    for piece in range(down_rows // extra):
        out_ref[2 * tokens :, down_rows:, piece * rest : (piece + 1) * rest] = down_ref[
            :, piece * extra : (piece + 1) * extra, hidden_width:
        ]


def pack_weights(w_gate, w_up, w_down):
    tokens, part_rows, hidden_width = w_gate.shape
    return pl.pallas_call(
        pack_kernel,
        out_shape=jax.ShapeDtypeStruct((3 * tokens, part_rows, hidden_width), jnp.bfloat16),
    )(w_gate, w_up, w_down)


def shards(table, hist_owner, hist_row, hist_len, w_in, queries, ffn_gain, w_gate, w_up, w_down):
    ntok = lax.axis_size("tok")
    nbatch = lax.axis_size("batch")
    devices = ntok * nbatch
    users, slots = hist_row.shape
    emb = table.shape[1]
    width = w_in.shape[1]
    nquery = queries.shape[0]
    headsz = width // nquery
    count = users * slots
    cap = 2 * count // devices
    weights = lax.all_gather(pack_weights(w_gate, w_up, w_down)[None], "batch", axis=0, tiled=True)

    owners = hist_owner.reshape(count)
    places = jnp.arange(count, dtype=jnp.int32)
    same = (owners[:, None] == owners[None, :]) & (places[None, :] < places[:, None])
    rank = jnp.sum(same.astype(jnp.int32), axis=1)
    position = owners * cap + rank
    spots = jnp.arange(devices * cap, dtype=jnp.int32)
    request = jnp.sum(
        jnp.where(position[:, None] == spots[None, :], hist_row.reshape(count)[:, None], 0), axis=0
    )
    asked = lax.all_to_all(request.reshape(ntok, nbatch * cap), "tok", 0, 0, tiled=True)
    asked = asked.reshape(ntok, nbatch, cap).transpose(1, 0, 2).reshape(nbatch, ntok * cap)
    asked = lax.all_to_all(asked, "batch", 0, 0, tiled=True)
    wanted = asked.reshape(nbatch, ntok, cap).transpose(1, 0, 2).reshape(devices * cap)
    local = jnp.arange(table.shape[0], dtype=jnp.int32)
    served = jnp.dot(
        (wanted[:, None] == local[None, :]).astype(jnp.bfloat16),
        table,
        preferred_element_type=jnp.bfloat16,
    )
    answers = lax.all_to_all(
        served.reshape(devices, cap, emb), ("tok", "batch"), 0, 0, tiled=True
    ).reshape(devices * cap, emb)
    pooled = pool(hist_len, answers, position.reshape(count, 1), w_in, queries)
    mixed = lax.all_to_all(pooled, "tok", 0, 0, tiled=True)
    group = users * ntok
    tokens = nquery // ntok
    sent = net(mixed.reshape(group * tokens, width), ffn_gain, weights, ntok)
    back = lax.all_to_all(sent, "tok", 0, 0, tiled=True)
    return back.transpose(4, 1, 0, 2, 3).reshape(group, tokens, width)


def solution(mesh):
    placed = (
        P(("tok", "batch"), None),
        P(("batch", "tok"), None, None),
        P(("batch", "tok"), None),
        P(("batch", "tok")),
        P(),
        P(),
        P("tok", None),
        P("tok", "batch", None),
        P("tok", "batch", None),
        P("tok", "batch", None),
    )
    return jax.shard_map(
        shards, mesh=mesh, in_specs=placed, out_specs=P("batch", "tok", None), check_vma=False
    )
```

```python
import jax
import jax.numpy as jnp
from jax import lax
from jax.experimental import pallas as pl
from jax.experimental.pallas import tpu as pltpu
from jax.sharding import PartitionSpec as P

HEADS_STEP = 8
INNER = 8
MASKED = -1e30
LOG2E = 1.4426950408889634
EPS = 1e-06
CAP = 2
VMEM_BYTES = 50 * 1024 * 1024


def dot32(left, right):
    return jnp.dot(left, right, preferred_element_type=jnp.float32)


def one_hot(index, width):
    lanes = lax.broadcasted_iota(jnp.int32, (index.shape[0], width), 1)
    return jnp.where(lanes == index, 1.0, 0.0).astype(jnp.bfloat16)


def pool_kernel(len_ref, answer_ref, position_ref, w_in_ref, query_ref, out_ref, keys_ref):
    users = len_ref.shape[0]
    slots = position_ref.shape[0] // users
    inner, step_width, nquery = query_ref.shape
    headsz = step_width // HEADS_STEP
    heads = HEADS_STEP // 2
    step = pl.program_id(0)

    @pl.when(step == 0)
    def _():
        for user in range(users):
            span = slice(user * slots, (user + 1) * slots)
            pick = one_hot(position_ref[span, :], answer_ref.shape[0])
            rows = dot32(pick, answer_ref[...]).astype(jnp.bfloat16)
            proj = dot32(rows, w_in_ref[...])
            scale = lax.rsqrt(jnp.mean(proj * proj, axis=-1, keepdims=True) + EPS)
            keys = (proj * scale).astype(jnp.bfloat16)
            for part in range(keys_ref.shape[0]):
                keys_ref[part, span, :] = keys[:, part * step_width : (part + 1) * step_width]

    for sub in range(inner):
        query = query_ref[sub].astype(jnp.float32)
        wide = jnp.concatenate([query] * heads, axis=1)
        row_head = lax.broadcasted_iota(jnp.int32, wide.shape, 0) // headsz
        col_head = lax.broadcasted_iota(jnp.int32, wide.shape, 1) // nquery
        blocks = {}
        for half in range(2):
            spread = jnp.where(row_head == col_head + half * heads, wide, 0.0).astype(jnp.bfloat16)
            for user in range(users):
                keys = keys_ref[step * inner + sub, user * slots : (user + 1) * slots, :]
                scores = dot32(keys, spread)
                slot = lax.broadcasted_iota(jnp.int32, scores.shape, 0)
                scores = jnp.where(slot < len_ref[user], scores, MASKED)
                top = jnp.max(scores, axis=0, keepdims=True)
                weight = jnp.exp2((scores - top) * (LOG2E / headsz**0.5))
                total = jnp.sum(weight, axis=0, keepdims=True)
                attn = (weight * (1.0 / total)).astype(jnp.bfloat16)
                pooled = lax.dot_general(
                    keys, attn, (((0,), (0,)), ((), ())), preferred_element_type=jnp.float32
                )
                for head in range(heads):
                    at = (half * heads + head) * headsz
                    block = pooled[at : at + headsz, head * nquery : (head + 1) * nquery]
                    low = block[: headsz // 2, :]
                    high = block[headsz // 2 :, :]
                    blocks[user, half * heads + head] = jnp.concatenate([low, high], axis=1)
        for pair in range(heads):
            stack = jnp.stack(
                [blocks[user, 2 * pair + which] for user in range(users) for which in range(2)],
                axis=0,
            )
            turned = jnp.swapaxes(stack, 0, 1)
            row = jnp.concatenate([turned[part] for part in range(turned.shape[0])], axis=1)
            out_ref[sub * heads + pair, :, :] = row.astype(jnp.bfloat16)


def pool(lengths, answers, position, w_in, queries):
    users = lengths.shape[0]
    width = w_in.shape[1]
    nquery = queries.shape[0]
    parts = nquery // HEADS_STEP
    step_width = width // parts
    query_t = queries.T.reshape(parts, step_width, nquery)
    pairs = nquery // 2
    return pl.pallas_call(
        pool_kernel,
        grid=(parts // INNER,),
        in_specs=[
            pl.BlockSpec(memory_space=pltpu.SMEM),
            pl.BlockSpec(answers.shape, lambda i: (0, 0)),
            pl.BlockSpec(position.shape, lambda i: (0, 0)),
            pl.BlockSpec(w_in.shape, lambda i: (0, 0)),
            pl.BlockSpec((INNER, step_width, nquery), lambda i: (i, 0, 0)),
        ],
        out_specs=pl.BlockSpec((INNER * HEADS_STEP // 2, 2 * users, width), lambda i: (i, 0, 0)),
        out_shape=jax.ShapeDtypeStruct((pairs, 2 * users, width), jnp.bfloat16),
        scratch_shapes=[pltpu.VMEM((parts, position.shape[0], step_width), jnp.bfloat16)],
        compiler_params=pltpu.CompilerParams(vmem_limit_bytes=VMEM_BYTES),
    )(lengths, answers, position, w_in, query_t)


def net_kernel(mixed_ref, gain_ref, weight_ref, out_ref, gate_ref, up_ref, down_ref, sems):
    tokens = gain_ref.shape[0]
    rows, width = mixed_ref.shape
    group = rows // tokens
    nparts, _, part_rows, hidden_width = weight_ref.shape
    down_rows = down_ref.shape[2]
    rest = width - hidden_width
    headsz = out_ref.shape[3]
    copies = []
    for token in range(tokens):
        pieces = [
            (weight_ref.at[:, token, :, :], gate_ref.at[token]),
            (weight_ref.at[:, tokens + token, :, :], up_ref.at[token]),
            (
                weight_ref.at[:, 2 * tokens + token, pl.ds(0, down_rows), :],
                down_ref.at[token, :, :, pl.ds(0, hidden_width)],
            ),
        ]
        extra = part_rows - down_rows
        for piece in range(down_rows // extra):
            pieces.append(
                (
                    weight_ref.at[
                        :, 2 * tokens + token, pl.ds(down_rows, extra), pl.ds(piece * rest, rest)
                    ],
                    down_ref.at[token, :, pl.ds(piece * extra, extra), pl.ds(hidden_width, rest)],
                )
            )
        copies.append(
            [
                pltpu.make_async_copy(src, dst, sems.at[token, number])
                for number, (src, dst) in enumerate(pieces)
            ]
        )
    for some in copies:
        for copy in some:
            copy.start()
    target = lax.broadcasted_iota(jnp.int32, (rows, 1), 0)
    order = (target % group) * tokens + target // group
    sorted_rows = dot32(one_hot(order, rows), mixed_ref[...]).astype(jnp.bfloat16)
    nquery = width // headsz
    spot = lax.broadcasted_iota(jnp.int32, (width, 1), 0)
    feature = spot % nquery * headsz + (spot // nquery % 2) * (headsz // 2) + spot // (2 * nquery)
    mixed = dot32(sorted_rows, one_hot(feature, width))
    for token in range(tokens):
        wide = mixed[token * group : (token + 1) * group, :]
        scale = lax.rsqrt(jnp.mean(wide * wide, axis=-1, keepdims=True) + EPS)
        normed = (wide * scale * gain_ref[token : token + 1, :]).astype(jnp.bfloat16)
        copies[token][0].wait()
        gate = dot32(normed, gate_ref[token].reshape(width, hidden_width))
        copies[token][1].wait()
        up_val = dot32(normed, up_ref[token].reshape(width, hidden_width))
        hidden = (gate / (1.0 + jnp.exp(-gate)) * up_val).astype(jnp.bfloat16)
        for copy in copies[token][2:]:
            copy.wait()
        down = dot32(hidden, down_ref[token].reshape(hidden_width, width))
        summed = (wide + down).T.astype(jnp.bfloat16)
        out_ref[:, :, token, :, :] = summed.reshape(
            out_ref.shape[0], out_ref.shape[1], headsz, group
        )


def net(mixed, gain, weights, ntok):
    rows, width = mixed.shape
    tokens = gain.shape[0]
    group = rows // tokens
    nparts, _, part_rows, hidden_width = weights.shape
    down_rows = hidden_width // nparts
    nquery = ntok * tokens
    pieces = 3 + down_rows // (part_rows - down_rows)
    return pl.pallas_call(
        net_kernel,
        in_specs=[
            pl.BlockSpec(memory_space=pltpu.VMEM),
            pl.BlockSpec(memory_space=pltpu.VMEM),
            pl.BlockSpec(memory_space=pl.ANY),
        ],
        out_specs=pl.BlockSpec(memory_space=pltpu.VMEM),
        out_shape=jax.ShapeDtypeStruct(
            (ntok, tokens, tokens, width // nquery, group), jnp.bfloat16
        ),
        scratch_shapes=[
            pltpu.VMEM((tokens, nparts, part_rows, hidden_width), jnp.bfloat16),
            pltpu.VMEM((tokens, nparts, part_rows, hidden_width), jnp.bfloat16),
            pltpu.VMEM((tokens, nparts, down_rows, width), jnp.bfloat16),
            pltpu.SemaphoreType.DMA((tokens, pieces)),
        ],
        compiler_params=pltpu.CompilerParams(vmem_limit_bytes=VMEM_BYTES),
    )(mixed, gain, weights)


def ask_kernel(
    owner_ref, row_ref, gate_ref, up_ref, down_ref, packed_ref, request_ref, position_ref
):
    users, slots = owner_ref.shape
    ntok, wide = request_ref.shape
    owner_rows = owner_ref[...].astype(jnp.float32)
    owner_cols, row_cols, positions = [], [], []
    for user in range(users):
        owner_cols.append(jnp.broadcast_to(owner_rows[user : user + 1, :], (slots, slots)).T)
        row = row_ref[user : user + 1, :].astype(jnp.float32)
        row_cols.append(jnp.broadcast_to(row, (slots, slots)).T[:, :1].astype(jnp.int32))
    earlier = lax.broadcasted_iota(jnp.int32, (slots, slots), 1) < lax.broadcasted_iota(
        jnp.int32, (slots, slots), 0
    )
    for user in range(users):
        same = jnp.where(
            earlier & (owner_cols[user] == owner_rows[user : user + 1, :]), 1.0, 0.0
        )
        for other in range(user):
            same += jnp.where(owner_cols[user] == owner_rows[other : other + 1, :], 1.0, 0.0)
        rank = jnp.sum(same, axis=1, keepdims=True)
        positions.append((owner_cols[user][:, :1] * CAP + rank).astype(jnp.int32))
    position = jnp.concatenate(positions, axis=0)
    position_ref[...] = position
    rows = jnp.concatenate(row_cols, axis=0)
    lanes = lax.broadcasted_iota(jnp.int32, (position.shape[0], wide), 1)
    tall = lax.broadcasted_iota(jnp.int32, (position.shape[0], ntok), 1) == position // wide
    high = jnp.where(tall, (rows // 32).astype(jnp.float32), 0.0).astype(jnp.bfloat16)
    low = jnp.where(tall, (rows % 32).astype(jnp.float32), 0.0).astype(jnp.bfloat16)
    spot = jnp.where(lanes == position % wide, 1.0, 0.0).astype(jnp.bfloat16)
    both = (((0,), (0,)), ((), ()))
    asked_high = lax.dot_general(high, spot, both, preferred_element_type=jnp.float32)
    asked_low = lax.dot_general(low, spot, both, preferred_element_type=jnp.float32)
    request_ref[...] = (asked_high * 32.0 + asked_low).astype(jnp.int32)

    tokens, part_rows, hidden_width = gate_ref.shape
    _, down_rows, width = down_ref.shape
    rest = width - hidden_width
    extra = part_rows - down_rows
    packed_ref[:tokens] = gate_ref[...]
    packed_ref[tokens : 2 * tokens] = up_ref[...]
    packed_ref[2 * tokens :, :down_rows, :] = down_ref[:, :, :hidden_width]
    for piece in range(down_rows // extra):
        packed_ref[2 * tokens :, down_rows:, piece * rest : (piece + 1) * rest] = down_ref[
            :, piece * extra : (piece + 1) * extra, hidden_width:
        ]


def ask(owners, rows, w_gate, w_up, w_down, ntok, nbatch):
    tokens, part_rows, hidden_width = w_gate.shape
    return pl.pallas_call(
        ask_kernel,
        out_shape=[
            jax.ShapeDtypeStruct((3 * tokens, part_rows, hidden_width), jnp.bfloat16),
            jax.ShapeDtypeStruct((ntok, nbatch * CAP), jnp.int32),
            jax.ShapeDtypeStruct((owners.size, 1), jnp.int32),
        ],
    )(owners, rows, w_gate, w_up, w_down)


def shards(table, hist_owner, hist_row, hist_len, w_in, queries, ffn_gain, w_gate, w_up, w_down):
    ntok = lax.axis_size("tok")
    nbatch = lax.axis_size("batch")
    devices = ntok * nbatch
    users, slots = hist_row.shape
    emb = table.shape[1]
    width = w_in.shape[1]
    nquery = queries.shape[0]
    headsz = width // nquery
    cap = CAP
    packed, request, position = ask(
        hist_owner.reshape(users, slots), hist_row, w_gate, w_up, w_down, ntok, nbatch
    )
    weights = lax.all_gather(packed[None], "batch", axis=0, tiled=True)
    asked = lax.all_to_all(request, "tok", 0, 0, tiled=True)
    asked = asked.reshape(ntok, nbatch, cap).transpose(1, 0, 2).reshape(nbatch, ntok * cap)
    asked = lax.all_to_all(asked, "batch", 0, 0, tiled=True)
    wanted = asked.reshape(nbatch, ntok, cap).transpose(1, 0, 2).reshape(devices * cap)
    local = jnp.arange(table.shape[0], dtype=jnp.int32)
    served = jnp.dot(
        (wanted[:, None] == local[None, :]).astype(jnp.bfloat16),
        table,
        preferred_element_type=jnp.bfloat16,
    )
    answers = lax.all_to_all(
        served.reshape(devices, cap, emb), ("tok", "batch"), 0, 0, tiled=True
    ).reshape(devices * cap, emb)
    pooled = pool(hist_len, answers, position, w_in, queries)
    mixed = lax.all_to_all(pooled, "tok", 0, 0, tiled=True)
    group = users * ntok
    tokens = nquery // ntok
    sent = net(mixed.reshape(group * tokens, width), ffn_gain, weights, ntok)
    back = lax.all_to_all(sent, "tok", 0, 0, tiled=True)
    return back.transpose(4, 1, 0, 2, 3).reshape(group, tokens, width)


def solution(mesh):
    placed = (
        P(("tok", "batch"), None),
        P(("batch", "tok"), None, None),
        P(("batch", "tok"), None),
        P(("batch", "tok")),
        P(),
        P(),
        P("tok", None),
        P("tok", "batch", None),
        P("tok", "batch", None),
        P("tok", "batch", None),
    )
    return jax.shard_map(
        shards, mesh=mesh, in_specs=placed, out_specs=P("batch", "tok", None), check_vma=False
    )
```

```python
import jax
import jax.numpy as jnp
from jax import lax
from jax.experimental import pallas as pl
from jax.experimental.pallas import tpu as pltpu
from jax.sharding import PartitionSpec as P

HEADS_STEP = 8
INNER = 8
MASKED = -1e30
LOG2E = 1.4426950408889634
EPS = 1e-06
CAP = 2
VMEM_BYTES = 50 * 1024 * 1024


def dot32(left, right):
    return jnp.dot(left, right, preferred_element_type=jnp.float32)


def one_hot(index, width):
    lanes = lax.broadcasted_iota(jnp.int32, (index.shape[0], width), 1)
    return jnp.where(lanes == index, 1.0, 0.0).astype(jnp.bfloat16)


def pool_kernel(len_ref, answer_ref, position_ref, w_in_ref, query_ref, out_ref, keys_ref):
    users = len_ref.shape[0]
    slots = position_ref.shape[1]
    inner, step_width, nquery = query_ref.shape
    headsz = step_width // HEADS_STEP
    heads = HEADS_STEP // 2
    step = pl.program_id(0)

    @pl.when(step == 0)
    def _():
        placed = position_ref[...].astype(jnp.float32)
        columns = jnp.concatenate([placed, placed], axis=0).T.astype(jnp.int32)
        for user in range(users):
            span = slice(user * slots, (user + 1) * slots)
            pick = one_hot(columns[:, user : user + 1], answer_ref.shape[0])
            rows = dot32(pick, answer_ref[...]).astype(jnp.bfloat16)
            proj = dot32(rows, w_in_ref[...])
            scale = lax.rsqrt(jnp.mean(proj * proj, axis=-1, keepdims=True) + EPS)
            keys = (proj * scale).astype(jnp.bfloat16)
            for part in range(keys_ref.shape[0]):
                keys_ref[part, span, :] = keys[:, part * step_width : (part + 1) * step_width]

    for sub in range(inner):
        query = query_ref[sub].astype(jnp.float32)
        wide = jnp.concatenate([query] * heads, axis=1)
        row_head = lax.broadcasted_iota(jnp.int32, wide.shape, 0) // headsz
        col_head = lax.broadcasted_iota(jnp.int32, wide.shape, 1) // nquery
        blocks = {}
        for half in range(2):
            spread = jnp.where(row_head == col_head + half * heads, wide, 0.0).astype(jnp.bfloat16)
            for user in range(users):
                keys = keys_ref[step * inner + sub, user * slots : (user + 1) * slots, :]
                scores = dot32(keys, spread)
                slot = lax.broadcasted_iota(jnp.int32, scores.shape, 0)
                scores = jnp.where(slot < len_ref[user], scores, MASKED)
                top = jnp.max(scores, axis=0, keepdims=True)
                weight = jnp.exp2((scores - top) * (LOG2E / headsz**0.5))
                total = jnp.sum(weight, axis=0, keepdims=True)
                attn = (weight * (1.0 / total)).astype(jnp.bfloat16)
                pooled = lax.dot_general(
                    keys, attn, (((0,), (0,)), ((), ())), preferred_element_type=jnp.float32
                )
                for head in range(heads):
                    at = (half * heads + head) * headsz
                    block = pooled[at : at + headsz, head * nquery : (head + 1) * nquery]
                    low = block[: headsz // 2, :]
                    high = block[headsz // 2 :, :]
                    blocks[user, half * heads + head] = jnp.concatenate([low, high], axis=1)
        for pair in range(heads):
            stack = jnp.stack(
                [blocks[user, 2 * pair + which] for user in range(users) for which in range(2)],
                axis=0,
            )
            turned = jnp.swapaxes(stack, 0, 1)
            row = jnp.concatenate([turned[part] for part in range(turned.shape[0])], axis=1)
            out_ref[sub * heads + pair, :, :] = row.astype(jnp.bfloat16)


def pool(lengths, answers, position, w_in, queries):
    users = lengths.shape[0]
    width = w_in.shape[1]
    nquery = queries.shape[0]
    parts = nquery // HEADS_STEP
    step_width = width // parts
    query_t = queries.T.reshape(parts, step_width, nquery)
    pairs = nquery // 2
    return pl.pallas_call(
        pool_kernel,
        grid=(parts // INNER,),
        in_specs=[
            pl.BlockSpec(memory_space=pltpu.SMEM),
            pl.BlockSpec(answers.shape, lambda i: (0, 0)),
            pl.BlockSpec(position.shape, lambda i: (0, 0)),
            pl.BlockSpec(w_in.shape, lambda i: (0, 0)),
            pl.BlockSpec((INNER, step_width, nquery), lambda i: (i, 0, 0)),
        ],
        out_specs=pl.BlockSpec((INNER * HEADS_STEP // 2, 2 * users, width), lambda i: (i, 0, 0)),
        out_shape=jax.ShapeDtypeStruct((pairs, 2 * users, width), jnp.bfloat16),
        scratch_shapes=[pltpu.VMEM((parts, position.size, step_width), jnp.bfloat16)],
        compiler_params=pltpu.CompilerParams(vmem_limit_bytes=VMEM_BYTES),
    )(lengths, answers, position, w_in, query_t)


def net_kernel(mixed_ref, gain_ref, weight_ref, out_ref, gate_ref, up_ref, down_ref, sems):
    tokens = gain_ref.shape[0]
    rows, width = mixed_ref.shape
    group = rows // tokens
    nparts, _, part_rows, hidden_width = weight_ref.shape
    down_rows = down_ref.shape[2]
    rest = width - hidden_width
    headsz = out_ref.shape[3]
    copies = []
    for token in range(tokens):
        pieces = [
            (weight_ref.at[:, token, :, :], gate_ref.at[token]),
            (weight_ref.at[:, tokens + token, :, :], up_ref.at[token]),
            (
                weight_ref.at[:, 2 * tokens + token, pl.ds(0, down_rows), :],
                down_ref.at[token, :, :, pl.ds(0, hidden_width)],
            ),
        ]
        extra = part_rows - down_rows
        for piece in range(down_rows // extra):
            pieces.append(
                (
                    weight_ref.at[
                        :, 2 * tokens + token, pl.ds(down_rows, extra), pl.ds(piece * rest, rest)
                    ],
                    down_ref.at[token, :, pl.ds(piece * extra, extra), pl.ds(hidden_width, rest)],
                )
            )
        copies.append(
            [
                pltpu.make_async_copy(src, dst, sems.at[token, number])
                for number, (src, dst) in enumerate(pieces)
            ]
        )
    for some in copies:
        for copy in some:
            copy.start()
    target = lax.broadcasted_iota(jnp.int32, (rows, 1), 0)
    order = (target % group) * tokens + target // group
    sorted_rows = dot32(one_hot(order, rows), mixed_ref[...]).astype(jnp.bfloat16)
    nquery = width // headsz
    spot = lax.broadcasted_iota(jnp.int32, (width, 1), 0)
    feature = spot % nquery * headsz + (spot // nquery % 2) * (headsz // 2) + spot // (2 * nquery)
    mixed = dot32(sorted_rows, one_hot(feature, width))
    for token in range(tokens):
        wide = mixed[token * group : (token + 1) * group, :]
        scale = lax.rsqrt(jnp.mean(wide * wide, axis=-1, keepdims=True) + EPS)
        normed = (wide * scale * gain_ref[token : token + 1, :]).astype(jnp.bfloat16)
        copies[token][0].wait()
        gate = dot32(normed, gate_ref[token].reshape(width, hidden_width))
        copies[token][1].wait()
        up_val = dot32(normed, up_ref[token].reshape(width, hidden_width))
        hidden = (gate / (1.0 + jnp.exp(-gate)) * up_val).astype(jnp.bfloat16)
        for copy in copies[token][2:]:
            copy.wait()
        down = dot32(hidden, down_ref[token].reshape(hidden_width, width))
        summed = (wide + down).T.astype(jnp.bfloat16)
        out_ref[:, :, token, :, :] = summed.reshape(
            out_ref.shape[0], out_ref.shape[1], headsz, group
        )


def net(mixed, gain, weights, ntok):
    rows, width = mixed.shape
    tokens = gain.shape[0]
    group = rows // tokens
    nparts, _, part_rows, hidden_width = weights.shape
    down_rows = hidden_width // nparts
    nquery = ntok * tokens
    pieces = 3 + down_rows // (part_rows - down_rows)
    return pl.pallas_call(
        net_kernel,
        in_specs=[
            pl.BlockSpec(memory_space=pltpu.VMEM),
            pl.BlockSpec(memory_space=pltpu.VMEM),
            pl.BlockSpec(memory_space=pl.ANY),
        ],
        out_specs=pl.BlockSpec(memory_space=pltpu.VMEM),
        out_shape=jax.ShapeDtypeStruct(
            (ntok, tokens, tokens, width // nquery, group), jnp.bfloat16
        ),
        scratch_shapes=[
            pltpu.VMEM((tokens, nparts, part_rows, hidden_width), jnp.bfloat16),
            pltpu.VMEM((tokens, nparts, part_rows, hidden_width), jnp.bfloat16),
            pltpu.VMEM((tokens, nparts, down_rows, width), jnp.bfloat16),
            pltpu.SemaphoreType.DMA((tokens, pieces)),
        ],
        compiler_params=pltpu.CompilerParams(vmem_limit_bytes=VMEM_BYTES),
    )(mixed, gain, weights)


def ask_kernel(
    owner_ref, row_ref, gate_ref, up_ref, down_ref, packed_ref, request_ref, position_ref
):
    users, slots = owner_ref.shape
    ntok, wide = request_ref.shape
    owner_rows = owner_ref[...].astype(jnp.float32)
    owner_cols = jnp.concatenate([owner_rows, owner_rows], axis=0).T
    earlier = lax.broadcasted_iota(jnp.int32, (slots, slots), 0) < lax.broadcasted_iota(
        jnp.int32, (slots, slots), 1
    )
    lanes = lax.broadcasted_iota(jnp.int32, (wide, slots), 0)
    groups = lax.broadcasted_iota(jnp.int32, (ntok, slots), 0)
    across = (((1,), (1,)), ((), ()))
    asked = jnp.zeros((ntok, wide), jnp.float32)
    positions = []
    for user in range(users):
        mine = owner_rows[user : user + 1, :]
        same = jnp.where(earlier & (owner_cols[:, user : user + 1] == mine), 1.0, 0.0)
        for other in range(user):
            same += jnp.where(owner_cols[:, other : other + 1] == mine, 1.0, 0.0)
        rank = jnp.sum(same, axis=0, keepdims=True)
        position = (mine * CAP + rank).astype(jnp.int32)
        positions.append(position)
        row = row_ref[user : user + 1, :]
        here = groups == position // wide
        high = jnp.where(here, (row // 32).astype(jnp.float32), 0.0).astype(jnp.bfloat16)
        low = jnp.where(here, (row % 32).astype(jnp.float32), 0.0).astype(jnp.bfloat16)
        spot = jnp.where(lanes == position % wide, 1.0, 0.0).astype(jnp.bfloat16)
        asked_high = lax.dot_general(high, spot, across, preferred_element_type=jnp.float32)
        asked_low = lax.dot_general(low, spot, across, preferred_element_type=jnp.float32)
        asked += asked_high * 32.0 + asked_low
    position_ref[...] = jnp.concatenate(positions, axis=0)
    request_ref[...] = asked.astype(jnp.int32)

    tokens, part_rows, hidden_width = gate_ref.shape
    _, down_rows, width = down_ref.shape
    rest = width - hidden_width
    extra = part_rows - down_rows
    packed_ref[:tokens] = gate_ref[...]
    packed_ref[tokens : 2 * tokens] = up_ref[...]
    packed_ref[2 * tokens :, :down_rows, :] = down_ref[:, :, :hidden_width]
    for piece in range(down_rows // extra):
        packed_ref[2 * tokens :, down_rows:, piece * rest : (piece + 1) * rest] = down_ref[
            :, piece * extra : (piece + 1) * extra, hidden_width:
        ]


def ask(owners, rows, w_gate, w_up, w_down, ntok, nbatch):
    tokens, part_rows, hidden_width = w_gate.shape
    return pl.pallas_call(
        ask_kernel,
        out_shape=[
            jax.ShapeDtypeStruct((3 * tokens, part_rows, hidden_width), jnp.bfloat16),
            jax.ShapeDtypeStruct((ntok, nbatch * CAP), jnp.int32),
            jax.ShapeDtypeStruct(owners.shape, jnp.int32),
        ],
    )(owners, rows, w_gate, w_up, w_down)


def shards(table, hist_owner, hist_row, hist_len, w_in, queries, ffn_gain, w_gate, w_up, w_down):
    ntok = lax.axis_size("tok")
    nbatch = lax.axis_size("batch")
    devices = ntok * nbatch
    users, slots = hist_row.shape
    emb = table.shape[1]
    width = w_in.shape[1]
    nquery = queries.shape[0]
    headsz = width // nquery
    cap = CAP
    packed, request, position = ask(
        hist_owner.reshape(users, slots), hist_row, w_gate, w_up, w_down, ntok, nbatch
    )
    weights = lax.all_gather(packed[None], "batch", axis=0, tiled=True)
    asked = lax.all_to_all(request, "tok", 0, 0, tiled=True)
    asked = asked.reshape(ntok, nbatch, cap).transpose(1, 0, 2).reshape(nbatch, ntok * cap)
    asked = lax.all_to_all(asked, "batch", 0, 0, tiled=True)
    wanted = asked.reshape(nbatch, ntok, cap).transpose(1, 0, 2).reshape(devices * cap)
    local = jnp.arange(table.shape[0], dtype=jnp.int32)
    served = jnp.dot(
        (wanted[:, None] == local[None, :]).astype(jnp.bfloat16),
        table,
        preferred_element_type=jnp.bfloat16,
    )
    answers = lax.all_to_all(
        served.reshape(devices, cap, emb), ("tok", "batch"), 0, 0, tiled=True
    ).reshape(devices * cap, emb)
    pooled = pool(hist_len, answers, position, w_in, queries)
    mixed = lax.all_to_all(pooled, "tok", 0, 0, tiled=True)
    group = users * ntok
    tokens = nquery // ntok
    sent = net(mixed.reshape(group * tokens, width), ffn_gain, weights, ntok)
    back = lax.all_to_all(sent, "tok", 0, 0, tiled=True)
    return back.transpose(4, 1, 0, 2, 3).reshape(group, tokens, width)


def solution(mesh):
    placed = (
        P(("tok", "batch"), None),
        P(("batch", "tok"), None, None),
        P(("batch", "tok"), None),
        P(("batch", "tok")),
        P(),
        P(),
        P("tok", None),
        P("tok", "batch", None),
        P("tok", "batch", None),
        P("tok", "batch", None),
    )
    return jax.shard_map(
        shards, mesh=mesh, in_specs=placed, out_specs=P("batch", "tok", None), check_vma=False
    )
```

```python
import jax
import jax.numpy as jnp
from jax import lax
from jax.experimental import pallas as pl
from jax.experimental.pallas import tpu as pltpu
from jax.sharding import PartitionSpec as P

HEADS_STEP = 8
INNER = 8
MASKED = -1e30
LOG2E = 1.4426950408889634
EPS = 1e-06
CAP = 2
VMEM_BYTES = 50 * 1024 * 1024


def dot32(left, right):
    return jnp.dot(left, right, preferred_element_type=jnp.float32)


def one_hot(index, width):
    lanes = lax.broadcasted_iota(jnp.int32, (index.shape[0], width), 1)
    return jnp.where(lanes == index, 1.0, 0.0).astype(jnp.bfloat16)


def pool_kernel(len_ref, answer_ref, position_ref, w_in_ref, query_ref, out_ref, keys_ref):
    users = len_ref.shape[0]
    slots = position_ref.shape[1]
    inner, step_width, nquery = query_ref.shape
    headsz = step_width // HEADS_STEP
    heads = HEADS_STEP // 2
    step = pl.program_id(0)

    @pl.when(step == 0)
    def _():
        placed = position_ref[...].astype(jnp.float32)
        columns = jnp.concatenate([placed, placed], axis=0).T.astype(jnp.int32)
        for user in range(users):
            span = slice(user * slots, (user + 1) * slots)
            pick = one_hot(columns[:, user : user + 1], answer_ref.shape[0])
            rows = dot32(pick, answer_ref[...]).astype(jnp.bfloat16)
            proj = dot32(rows, w_in_ref[...])
            scale = lax.rsqrt(jnp.mean(proj * proj, axis=-1, keepdims=True) + EPS)
            keys = (proj * scale).astype(jnp.bfloat16)
            for part in range(keys_ref.shape[0]):
                keys_ref[part, span, :] = keys[:, part * step_width : (part + 1) * step_width]

    for sub in range(inner):
        query = query_ref[sub].astype(jnp.float32)
        wide = jnp.concatenate([query] * heads, axis=1)
        row_head = lax.broadcasted_iota(jnp.int32, wide.shape, 0) // headsz
        col_head = lax.broadcasted_iota(jnp.int32, wide.shape, 1) // nquery
        blocks = {}
        for half in range(2):
            spread = jnp.where(row_head == col_head + half * heads, wide, 0.0).astype(jnp.bfloat16)
            for user in range(users):
                keys = keys_ref[step * inner + sub, user * slots : (user + 1) * slots, :]
                scores = dot32(keys, spread)
                slot = lax.broadcasted_iota(jnp.int32, scores.shape, 0)
                scores = jnp.where(slot < len_ref[user], scores, MASKED)
                top = jnp.max(scores, axis=0, keepdims=True)
                weight = jnp.exp2((scores - top) * (LOG2E / headsz**0.5))
                total = jnp.sum(weight, axis=0, keepdims=True)
                attn = (weight * (1.0 / total)).astype(jnp.bfloat16)
                pooled = lax.dot_general(
                    keys, attn, (((0,), (0,)), ((), ())), preferred_element_type=jnp.float32
                )
                for head in range(heads):
                    at = (half * heads + head) * headsz
                    block = pooled[at : at + headsz, head * nquery : (head + 1) * nquery]
                    low = block[: headsz // 2, :]
                    high = block[headsz // 2 :, :]
                    blocks[user, half * heads + head] = jnp.concatenate([low, high], axis=1)
        for pair in range(heads):
            stack = jnp.stack(
                [blocks[user, 2 * pair + which] for user in range(users) for which in range(2)],
                axis=0,
            )
            turned = jnp.swapaxes(stack, 0, 1)
            row = jnp.concatenate([turned[part] for part in range(turned.shape[0])], axis=1)
            out_ref[sub * heads + pair, :, :] = row.astype(jnp.bfloat16)


def pool(lengths, answers, position, w_in, queries):
    users = lengths.shape[0]
    width = w_in.shape[1]
    nquery = queries.shape[0]
    parts = nquery // HEADS_STEP
    step_width = width // parts
    query_t = queries.T.reshape(parts, step_width, nquery)
    pairs = nquery // 2
    return pl.pallas_call(
        pool_kernel,
        grid=(parts // INNER,),
        in_specs=[
            pl.BlockSpec(memory_space=pltpu.SMEM),
            pl.BlockSpec(answers.shape, lambda i: (0, 0)),
            pl.BlockSpec(position.shape, lambda i: (0, 0)),
            pl.BlockSpec(w_in.shape, lambda i: (0, 0)),
            pl.BlockSpec((INNER, step_width, nquery), lambda i: (i, 0, 0)),
        ],
        out_specs=pl.BlockSpec((INNER * HEADS_STEP // 2, 2 * users, width), lambda i: (i, 0, 0)),
        out_shape=jax.ShapeDtypeStruct((pairs, 2 * users, width), jnp.bfloat16),
        scratch_shapes=[pltpu.VMEM((parts, position.size, step_width), jnp.bfloat16)],
        compiler_params=pltpu.CompilerParams(vmem_limit_bytes=VMEM_BYTES),
    )(lengths, answers, position, w_in, query_t)


def net_kernel(mixed_ref, gain_ref, weight_ref, out_ref, held_ref, sems):
    tokens = gain_ref.shape[0]
    rows, width = mixed_ref.shape
    group = rows // tokens
    _, nparts, _, part_rows, hidden_width = held_ref.shape
    down_rows = hidden_width // nparts
    rest = width - hidden_width
    extra = part_rows - down_rows
    headsz = out_ref.shape[3]
    copies = [
        [
            pltpu.make_async_copy(
                weight_ref.at[:, token, pl.ds(first, some)],
                held_ref.at[token, :, pl.ds(first, some)],
                sems.at[token, number],
            )
            for number, (first, some) in enumerate(((0, 2), (2, 1)))
        ]
        for token in range(tokens)
    ]
    for some in copies:
        for copy in some:
            copy.start()
    target = lax.broadcasted_iota(jnp.int32, (rows, 1), 0)
    order = (target % group) * tokens + target // group
    sorted_rows = dot32(one_hot(order, rows), mixed_ref[...]).astype(jnp.bfloat16)
    nquery = width // headsz
    spot = lax.broadcasted_iota(jnp.int32, (width, 1), 0)
    feature = spot % nquery * headsz + (spot // nquery % 2) * (headsz // 2) + spot // (2 * nquery)
    mixed = dot32(sorted_rows, one_hot(feature, width))
    for token in range(tokens):
        wide = mixed[token * group : (token + 1) * group, :]
        scale = lax.rsqrt(jnp.mean(wide * wide, axis=-1, keepdims=True) + EPS)
        normed = (wide * scale * gain_ref[token : token + 1, :]).astype(jnp.bfloat16)
        copies[token][0].wait()
        gate = dot32(normed, held_ref[token, :, 0].reshape(width, hidden_width))
        up_val = dot32(normed, held_ref[token, :, 1].reshape(width, hidden_width))
        hidden = (gate / (1.0 + jnp.exp(-gate)) * up_val).astype(jnp.bfloat16)
        copies[token][1].wait()
        left = held_ref[token, :, 2, :down_rows, :].reshape(hidden_width, hidden_width)
        right = jnp.stack(
            [
                held_ref[token, :, 2, down_rows:, piece * rest : (piece + 1) * rest]
                for piece in range(down_rows // extra)
            ],
            axis=1,
        ).reshape(hidden_width, rest)
        down = jnp.concatenate([dot32(hidden, left), dot32(hidden, right)], axis=1)
        summed = (wide + down).T.astype(jnp.bfloat16)
        out_ref[:, :, token, :, :] = summed.reshape(
            out_ref.shape[0], out_ref.shape[1], headsz, group
        )


def net(mixed, gain, weights, ntok):
    rows, width = mixed.shape
    tokens = gain.shape[0]
    group = rows // tokens
    nparts, _, kinds, part_rows, hidden_width = weights.shape
    nquery = ntok * tokens
    return pl.pallas_call(
        net_kernel,
        in_specs=[
            pl.BlockSpec(memory_space=pltpu.VMEM),
            pl.BlockSpec(memory_space=pltpu.VMEM),
            pl.BlockSpec(memory_space=pl.ANY),
        ],
        out_specs=pl.BlockSpec(memory_space=pltpu.VMEM),
        out_shape=jax.ShapeDtypeStruct(
            (ntok, tokens, tokens, width // nquery, group), jnp.bfloat16
        ),
        scratch_shapes=[
            pltpu.VMEM((tokens, nparts, kinds, part_rows, hidden_width), jnp.bfloat16),
            pltpu.SemaphoreType.DMA((tokens, 2)),
        ],
        compiler_params=pltpu.CompilerParams(vmem_limit_bytes=VMEM_BYTES),
    )(mixed, gain, weights)


def ask_kernel(
    owner_ref, row_ref, gate_ref, up_ref, down_ref, packed_ref, request_ref, position_ref
):
    users, slots = owner_ref.shape
    ntok, wide = request_ref.shape
    owner_rows = owner_ref[...].astype(jnp.float32)
    owner_cols = jnp.concatenate([owner_rows, owner_rows], axis=0).T
    earlier = lax.broadcasted_iota(jnp.int32, (slots, slots), 0) < lax.broadcasted_iota(
        jnp.int32, (slots, slots), 1
    )
    lanes = lax.broadcasted_iota(jnp.int32, (wide, slots), 0)
    groups = lax.broadcasted_iota(jnp.int32, (ntok, slots), 0)
    across = (((1,), (1,)), ((), ()))
    asked = jnp.zeros((ntok, wide), jnp.float32)
    positions = []
    for user in range(users):
        mine = owner_rows[user : user + 1, :]
        same = jnp.where(earlier & (owner_cols[:, user : user + 1] == mine), 1.0, 0.0)
        for other in range(user):
            same += jnp.where(owner_cols[:, other : other + 1] == mine, 1.0, 0.0)
        rank = jnp.sum(same, axis=0, keepdims=True)
        position = (mine * CAP + rank).astype(jnp.int32)
        positions.append(position)
        row = row_ref[user : user + 1, :]
        here = groups == position // wide
        high = jnp.where(here, (row // 32).astype(jnp.float32), 0.0).astype(jnp.bfloat16)
        low = jnp.where(here, (row % 32).astype(jnp.float32), 0.0).astype(jnp.bfloat16)
        spot = jnp.where(lanes == position % wide, 1.0, 0.0).astype(jnp.bfloat16)
        asked_high = lax.dot_general(high, spot, across, preferred_element_type=jnp.float32)
        asked_low = lax.dot_general(low, spot, across, preferred_element_type=jnp.float32)
        asked += asked_high * 32.0 + asked_low
    position_ref[...] = jnp.concatenate(positions, axis=0)
    request_ref[...] = asked.astype(jnp.int32)

    tokens, part_rows, hidden_width = gate_ref.shape
    _, down_rows, width = down_ref.shape
    rest = width - hidden_width
    extra = part_rows - down_rows
    for token in range(tokens):
        packed_ref[token, 0] = gate_ref[token]
        packed_ref[token, 1] = up_ref[token]
        packed_ref[token, 2, :down_rows, :] = down_ref[token, :, :hidden_width]
        for piece in range(down_rows // extra):
            packed_ref[token, 2, down_rows:, piece * rest : (piece + 1) * rest] = down_ref[
                token, piece * extra : (piece + 1) * extra, hidden_width:
            ]


def ask(owners, rows, w_gate, w_up, w_down, ntok, nbatch):
    tokens, part_rows, hidden_width = w_gate.shape
    return pl.pallas_call(
        ask_kernel,
        out_shape=[
            jax.ShapeDtypeStruct((tokens, 3, part_rows, hidden_width), jnp.bfloat16),
            jax.ShapeDtypeStruct((ntok, nbatch * CAP), jnp.int32),
            jax.ShapeDtypeStruct(owners.shape, jnp.int32),
        ],
    )(owners, rows, w_gate, w_up, w_down)


def shards(table, hist_owner, hist_row, hist_len, w_in, queries, ffn_gain, w_gate, w_up, w_down):
    ntok = lax.axis_size("tok")
    nbatch = lax.axis_size("batch")
    devices = ntok * nbatch
    users, slots = hist_row.shape
    emb = table.shape[1]
    width = w_in.shape[1]
    nquery = queries.shape[0]
    headsz = width // nquery
    cap = CAP
    packed, request, position = ask(
        hist_owner.reshape(users, slots), hist_row, w_gate, w_up, w_down, ntok, nbatch
    )
    weights = lax.all_gather(packed[None], "batch", axis=0, tiled=True)
    asked = lax.all_to_all(request, "tok", 0, 0, tiled=True)
    asked = asked.reshape(ntok, nbatch, cap).transpose(1, 0, 2).reshape(nbatch, ntok * cap)
    asked = lax.all_to_all(asked, "batch", 0, 0, tiled=True)
    wanted = asked.reshape(nbatch, ntok, cap).transpose(1, 0, 2).reshape(devices * cap)
    local = jnp.arange(table.shape[0], dtype=jnp.int32)
    served = jnp.dot(
        (wanted[:, None] == local[None, :]).astype(jnp.bfloat16),
        table,
        preferred_element_type=jnp.bfloat16,
    )
    answers = lax.all_to_all(
        served.reshape(devices, cap, emb), ("tok", "batch"), 0, 0, tiled=True
    ).reshape(devices * cap, emb)
    pooled = pool(hist_len, answers, position, w_in, queries)
    mixed = lax.all_to_all(pooled, "tok", 0, 0, tiled=True)
    group = users * ntok
    tokens = nquery // ntok
    sent = net(mixed.reshape(group * tokens, width), ffn_gain, weights, ntok)
    back = lax.all_to_all(sent, "tok", 0, 0, tiled=True)
    return back.transpose(4, 1, 0, 2, 3).reshape(group, tokens, width)


def solution(mesh):
    placed = (
        P(("tok", "batch"), None),
        P(("batch", "tok"), None, None),
        P(("batch", "tok"), None),
        P(("batch", "tok")),
        P(),
        P(),
        P("tok", None),
        P("tok", "batch", None),
        P("tok", "batch", None),
        P("tok", "batch", None),
    )
    return jax.shard_map(
        shards, mesh=mesh, in_specs=placed, out_specs=P("batch", "tok", None), check_vma=False
    )
```

```python
import jax
import jax.numpy as jnp
from jax import lax
from jax.experimental import pallas as pl
from jax.experimental.pallas import tpu as pltpu
from jax.sharding import PartitionSpec as P

HEADS_STEP = 8
INNER = 8
MASKED = -1e30
LOG2E = 1.4426950408889634
EPS = 1e-06
CAP = 2
VMEM_BYTES = 50 * 1024 * 1024


def dot32(left, right):
    return jnp.dot(left, right, preferred_element_type=jnp.float32)


def one_hot(index, width):
    lanes = lax.broadcasted_iota(jnp.int32, (index.shape[0], width), 1)
    return jnp.where(lanes == index, 1.0, 0.0).astype(jnp.bfloat16)


def pool_kernel(len_ref, answer_ref, position_ref, w_in_ref, query_ref, out_ref, keys_ref):
    users = len_ref.shape[0]
    slots = position_ref.shape[1]
    inner, step_width, nquery = query_ref.shape
    headsz = step_width // HEADS_STEP
    heads = HEADS_STEP // 2
    step = pl.program_id(0)

    @pl.when(step == 0)
    def _():
        placed = position_ref[...].astype(jnp.float32)
        columns = jnp.concatenate([placed, placed], axis=0).T.astype(jnp.int32)
        for user in range(users):
            span = slice(user * slots, (user + 1) * slots)
            pick = one_hot(columns[:, user : user + 1], answer_ref.shape[0])
            rows = dot32(pick, answer_ref[...]).astype(jnp.bfloat16)
            proj = dot32(rows, w_in_ref[...])
            scale = lax.rsqrt(jnp.mean(proj * proj, axis=-1, keepdims=True) + EPS)
            keys = (proj * scale).astype(jnp.bfloat16)
            for part in range(keys_ref.shape[0]):
                keys_ref[part, span, :] = keys[:, part * step_width : (part + 1) * step_width]

    for sub in range(inner):
        query = query_ref[sub].astype(jnp.float32)
        wide = jnp.concatenate([query] * heads, axis=1)
        row_head = lax.broadcasted_iota(jnp.int32, wide.shape, 0) // headsz
        col_head = lax.broadcasted_iota(jnp.int32, wide.shape, 1) // nquery
        blocks = {}
        for half in range(2):
            spread = jnp.where(row_head == col_head + half * heads, wide, 0.0).astype(jnp.bfloat16)
            for user in range(users):
                keys = keys_ref[step * inner + sub, user * slots : (user + 1) * slots, :]
                scores = dot32(keys, spread)
                slot = lax.broadcasted_iota(jnp.int32, scores.shape, 0)
                scores = jnp.where(slot < len_ref[user], scores, MASKED)
                top = jnp.max(scores, axis=0, keepdims=True)
                weight = jnp.exp2((scores - top) * (LOG2E / headsz**0.5))
                total = jnp.sum(weight, axis=0, keepdims=True)
                attn = (weight * (1.0 / total)).astype(jnp.bfloat16)
                pooled = lax.dot_general(
                    keys, attn, (((0,), (0,)), ((), ())), preferred_element_type=jnp.float32
                )
                for head in range(heads):
                    at = (half * heads + head) * headsz
                    block = pooled[at : at + headsz, head * nquery : (head + 1) * nquery]
                    low = block[: headsz // 2, :]
                    high = block[headsz // 2 :, :]
                    blocks[user, half * heads + head] = jnp.concatenate([low, high], axis=1)
        for pair in range(heads):
            stack = jnp.stack(
                [blocks[user, 2 * pair + which] for user in range(users) for which in range(2)],
                axis=0,
            )
            turned = jnp.swapaxes(stack, 0, 1)
            row = jnp.concatenate([turned[part] for part in range(turned.shape[0])], axis=1)
            out_ref[sub * heads + pair, :, :] = row.astype(jnp.bfloat16)


def pool(lengths, answers, position, w_in, queries):
    users = lengths.shape[0]
    width = w_in.shape[1]
    nquery = queries.shape[0]
    parts = nquery // HEADS_STEP
    step_width = width // parts
    query_t = queries.T.reshape(parts, step_width, nquery)
    pairs = nquery // 2
    return pl.pallas_call(
        pool_kernel,
        grid=(parts // INNER,),
        in_specs=[
            pl.BlockSpec(memory_space=pltpu.SMEM),
            pl.BlockSpec(answers.shape, lambda i: (0, 0)),
            pl.BlockSpec(position.shape, lambda i: (0, 0)),
            pl.BlockSpec(w_in.shape, lambda i: (0, 0)),
            pl.BlockSpec((INNER, step_width, nquery), lambda i: (i, 0, 0)),
        ],
        out_specs=pl.BlockSpec((INNER * HEADS_STEP // 2, 2 * users, width), lambda i: (i, 0, 0)),
        out_shape=jax.ShapeDtypeStruct((pairs, 2 * users, width), jnp.bfloat16),
        scratch_shapes=[pltpu.VMEM((parts, position.size, step_width), jnp.bfloat16)],
        compiler_params=pltpu.CompilerParams(vmem_limit_bytes=VMEM_BYTES),
    )(lengths, answers, position, w_in, query_t)


def net_kernel(mixed_ref, gain_ref, weight_ref, out_ref, gate_ref, up_ref, down_ref, sems):
    tokens = gain_ref.shape[0]
    rows, width = mixed_ref.shape
    group = rows // tokens
    nparts, _, part_rows, hidden_width = weight_ref.shape
    down_rows = down_ref.shape[2]
    rest = width - hidden_width
    headsz = out_ref.shape[3]
    copies = []
    for token in range(tokens):
        some = nparts // 2
        pieces = [
            (
                weight_ref.at[pl.ds(first, some), kind * tokens + token, :, :],
                into.at[token, pl.ds(first, some)],
            )
            for kind, into in enumerate((gate_ref, up_ref))
            for first in (0, some)
        ]
        pieces += [
            (
                weight_ref.at[:, 2 * tokens + token, pl.ds(0, down_rows), :],
                down_ref.at[token, :, :, pl.ds(0, hidden_width)],
            ),
        ]
        extra = part_rows - down_rows
        for piece in range(down_rows // extra):
            pieces.append(
                (
                    weight_ref.at[
                        :, 2 * tokens + token, pl.ds(down_rows, extra), pl.ds(piece * rest, rest)
                    ],
                    down_ref.at[token, :, pl.ds(piece * extra, extra), pl.ds(hidden_width, rest)],
                )
            )
        copies.append(
            [
                pltpu.make_async_copy(src, dst, sems.at[token, number])
                for number, (src, dst) in enumerate(pieces)
            ]
        )
    for some in copies:
        for copy in some:
            copy.start()
    target = lax.broadcasted_iota(jnp.int32, (rows, 1), 0)
    order = (target % group) * tokens + target // group
    sorted_rows = dot32(one_hot(order, rows), mixed_ref[...]).astype(jnp.bfloat16)
    nquery = width // headsz
    spot = lax.broadcasted_iota(jnp.int32, (width, 1), 0)
    feature = spot % nquery * headsz + (spot // nquery % 2) * (headsz // 2) + spot // (2 * nquery)
    mixed = dot32(sorted_rows, one_hot(feature, width))
    for token in range(tokens):
        wide = mixed[token * group : (token + 1) * group, :]
        scale = lax.rsqrt(jnp.mean(wide * wide, axis=-1, keepdims=True) + EPS)
        normed = (wide * scale * gain_ref[token : token + 1, :]).astype(jnp.bfloat16)
        for copy in copies[token][:2]:
            copy.wait()
        gate = dot32(normed, gate_ref[token].reshape(width, hidden_width))
        for copy in copies[token][2:4]:
            copy.wait()
        up_val = dot32(normed, up_ref[token].reshape(width, hidden_width))
        hidden = (gate / (1.0 + jnp.exp(-gate)) * up_val).astype(jnp.bfloat16)
        for copy in copies[token][4:]:
            copy.wait()
        down = dot32(hidden, down_ref[token].reshape(hidden_width, width))
        summed = (wide + down).T.astype(jnp.bfloat16)
        out_ref[:, :, token, :, :] = summed.reshape(
            out_ref.shape[0], out_ref.shape[1], headsz, group
        )


def net(mixed, gain, weights, ntok):
    rows, width = mixed.shape
    tokens = gain.shape[0]
    group = rows // tokens
    nparts, _, part_rows, hidden_width = weights.shape
    down_rows = hidden_width // nparts
    nquery = ntok * tokens
    pieces = 5 + down_rows // (part_rows - down_rows)
    return pl.pallas_call(
        net_kernel,
        in_specs=[
            pl.BlockSpec(memory_space=pltpu.VMEM),
            pl.BlockSpec(memory_space=pltpu.VMEM),
            pl.BlockSpec(memory_space=pl.ANY),
        ],
        out_specs=pl.BlockSpec(memory_space=pltpu.VMEM),
        out_shape=jax.ShapeDtypeStruct(
            (ntok, tokens, tokens, width // nquery, group), jnp.bfloat16
        ),
        scratch_shapes=[
            pltpu.VMEM((tokens, nparts, part_rows, hidden_width), jnp.bfloat16),
            pltpu.VMEM((tokens, nparts, part_rows, hidden_width), jnp.bfloat16),
            pltpu.VMEM((tokens, nparts, down_rows, width), jnp.bfloat16),
            pltpu.SemaphoreType.DMA((tokens, pieces)),
        ],
        compiler_params=pltpu.CompilerParams(vmem_limit_bytes=VMEM_BYTES),
    )(mixed, gain, weights)


def ask_kernel(
    owner_ref, row_ref, gate_ref, up_ref, down_ref, packed_ref, request_ref, position_ref
):
    users, slots = owner_ref.shape
    ntok, wide = request_ref.shape
    owner_rows = owner_ref[...].astype(jnp.float32)
    owner_cols = jnp.concatenate([owner_rows, owner_rows], axis=0).T
    earlier = lax.broadcasted_iota(jnp.int32, (slots, slots), 0) < lax.broadcasted_iota(
        jnp.int32, (slots, slots), 1
    )
    lanes = lax.broadcasted_iota(jnp.int32, (wide, slots), 0)
    groups = lax.broadcasted_iota(jnp.int32, (ntok, slots), 0)
    across = (((1,), (1,)), ((), ()))
    asked = jnp.zeros((ntok, wide), jnp.float32)
    positions = []
    for user in range(users):
        mine = owner_rows[user : user + 1, :]
        same = jnp.where(earlier & (owner_cols[:, user : user + 1] == mine), 1.0, 0.0)
        for other in range(user):
            same += jnp.where(owner_cols[:, other : other + 1] == mine, 1.0, 0.0)
        rank = jnp.sum(same, axis=0, keepdims=True)
        position = (mine * CAP + rank).astype(jnp.int32)
        positions.append(position)
        row = row_ref[user : user + 1, :]
        here = groups == position // wide
        high = jnp.where(here, (row // 32).astype(jnp.float32), 0.0).astype(jnp.bfloat16)
        low = jnp.where(here, (row % 32).astype(jnp.float32), 0.0).astype(jnp.bfloat16)
        spot = jnp.where(lanes == position % wide, 1.0, 0.0).astype(jnp.bfloat16)
        asked_high = lax.dot_general(high, spot, across, preferred_element_type=jnp.float32)
        asked_low = lax.dot_general(low, spot, across, preferred_element_type=jnp.float32)
        asked += asked_high * 32.0 + asked_low
    position_ref[...] = jnp.concatenate(positions, axis=0)
    request_ref[...] = asked.astype(jnp.int32)

    tokens, part_rows, hidden_width = gate_ref.shape
    _, down_rows, width = down_ref.shape
    rest = width - hidden_width
    extra = part_rows - down_rows
    packed_ref[:tokens] = gate_ref[...]
    packed_ref[tokens : 2 * tokens] = up_ref[...]
    packed_ref[2 * tokens :, :down_rows, :] = down_ref[:, :, :hidden_width]
    for piece in range(down_rows // extra):
        packed_ref[2 * tokens :, down_rows:, piece * rest : (piece + 1) * rest] = down_ref[
            :, piece * extra : (piece + 1) * extra, hidden_width:
        ]


def ask(owners, rows, w_gate, w_up, w_down, ntok, nbatch):
    tokens, part_rows, hidden_width = w_gate.shape
    return pl.pallas_call(
        ask_kernel,
        out_shape=[
            jax.ShapeDtypeStruct((3 * tokens, part_rows, hidden_width), jnp.bfloat16),
            jax.ShapeDtypeStruct((ntok, nbatch * CAP), jnp.int32),
            jax.ShapeDtypeStruct(owners.shape, jnp.int32),
        ],
    )(owners, rows, w_gate, w_up, w_down)


def shards(table, hist_owner, hist_row, hist_len, w_in, queries, ffn_gain, w_gate, w_up, w_down):
    ntok = lax.axis_size("tok")
    nbatch = lax.axis_size("batch")
    devices = ntok * nbatch
    users, slots = hist_row.shape
    emb = table.shape[1]
    width = w_in.shape[1]
    nquery = queries.shape[0]
    headsz = width // nquery
    cap = CAP
    packed, request, position = ask(
        hist_owner.reshape(users, slots), hist_row, w_gate, w_up, w_down, ntok, nbatch
    )
    weights = lax.all_gather(packed[None], "batch", axis=0, tiled=True)
    asked = lax.all_to_all(request, "tok", 0, 0, tiled=True)
    asked = asked.reshape(ntok, nbatch, cap).transpose(1, 0, 2).reshape(nbatch, ntok * cap)
    asked = lax.all_to_all(asked, "batch", 0, 0, tiled=True)
    wanted = asked.reshape(nbatch, ntok, cap).transpose(1, 0, 2).reshape(devices * cap)
    local = jnp.arange(table.shape[0], dtype=jnp.int32)
    served = jnp.dot(
        (wanted[:, None] == local[None, :]).astype(jnp.bfloat16),
        table,
        preferred_element_type=jnp.bfloat16,
    )
    answers = lax.all_to_all(
        served.reshape(devices, cap, emb), ("tok", "batch"), 0, 0, tiled=True
    ).reshape(devices * cap, emb)
    pooled = pool(hist_len, answers, position, w_in, queries)
    mixed = lax.all_to_all(pooled, "tok", 0, 0, tiled=True)
    group = users * ntok
    tokens = nquery // ntok
    sent = net(mixed.reshape(group * tokens, width), ffn_gain, weights, ntok)
    back = lax.all_to_all(sent, "tok", 0, 0, tiled=True)
    return back.transpose(4, 1, 0, 2, 3).reshape(group, tokens, width)


def solution(mesh):
    placed = (
        P(("tok", "batch"), None),
        P(("batch", "tok"), None, None),
        P(("batch", "tok"), None),
        P(("batch", "tok")),
        P(),
        P(),
        P("tok", None),
        P("tok", "batch", None),
        P("tok", "batch", None),
        P("tok", "batch", None),
    )
    return jax.shard_map(
        shards, mesh=mesh, in_specs=placed, out_specs=P("batch", "tok", None), check_vma=False
    )
```
